128 devices in a mesh: wide: 32 (over z, x, core), rhs: 4 (over y).
Axes of the slice: x: 4, y: 4, z: 4, core: 2. Of those that a mesh axis runs over, the one named last changes fastest.
Arguments:
- child_rhs: float32 [1024, 18432], P('rhs', 'wide'), may hold values from -6 to 6
- parent_rhs: float32 [1024, 12288], P('rhs', 'wide'), may hold values from -6 to 6
- child_inverse: bfloat16 [18432, 9216], P('wide'), as said below
- coupling: bfloat16 [18432, 3072], P('wide'), may hold values from -0.0625 to 0.0625
- parent_inverse: bfloat16 [12288, 12288], P('wide'), as said below
- child_blocks: int32 [2], replicated, may hold values from 36 to 72, as said below
- parent_block: int32 [2, 24], replicated, may hold values from 0 to 95, as said below
Outputs:
- child_solution: float32 [1024, 18432], P('rhs', 'wide')
- parent_solution: float32 [1024, 12288], P('rhs', 'wide')
The draws below stay inside these ranges and needn't reach their ends.
Inputs may be any that keep to these rules, and one draw needn't show every extreme that they name: `child_blocks`: one child has exactly 72 blocks, the other at least half of that. `parent_block`: the 24 entries of a row are distinct. `child_inverse`: lower triangular with unit diagonal. `parent_inverse`: lower triangular with unit diagonal.
All inputs are finite; a program needn't handle non-finite values.
Results may differ from the reference program's by a relative error of at most 0.0038.
Values may be sent and summed in bfloat16 or wider, within the bound.
No kernel may reach another device: no remote copies, remote signals or barrier semaphores. Data moves between devices by JAX's collectives and lax.ppermute only.
A program may use at most 192 MiB of HBM per device.

```python
import math
import jax
import jax.numpy as jnp

S0 = 12288
S1 = 9216
U = 3072
BLK = 128
NRHS = 1024


def lower_inverse(key, order, stacked):
    row_index = (jnp.arange(stacked * order) % order)[:, None]
    col_index = jnp.arange(order)[None, :]
    entries = jax.random.normal(key, (stacked * order, order), jnp.float32)
    entries = entries / math.sqrt(order)
    diagonal_part = jnp.where(col_index == row_index, 1.0, 0.0).astype(jnp.float32)
    return jnp.where(col_index < row_index, entries, diagonal_part).astype(jnp.bfloat16)


def draw_child_inverse(key, part):
    return lower_inverse(jax.random.fold_in(key, 11), S1, 2)


def draw_parent_inverse(key, part):
    return lower_inverse(jax.random.fold_in(key, 13), S0, 1)


def draw_child_blocks(key, part):
    full_key = jax.random.fold_in(key, 21)
    other_key = jax.random.fold_in(key, 22)
    which_full = jax.random.randint(full_key, (), 0, 2)
    smaller = jax.random.randint(other_key, (), S1 // (2 * BLK), S1 // BLK + 1)
    return jnp.where(jnp.arange(2) == which_full, S1 // BLK, smaller).astype(jnp.int32)


def draw_parent_block(key, part):
    block_total = S0 // BLK
    used_count = U // BLK
    first_row = jax.random.permutation(jax.random.fold_in(key, 31), block_total - 1)[:used_count - 1]
    first_row = jnp.concatenate([first_row, jnp.array([block_total - 1], jnp.int32)])
    second_row = 1 + jax.random.permutation(jax.random.fold_in(key, 32), block_total - 1)[:used_count - 1]
    second_row = jnp.concatenate([second_row, jnp.array([0], jnp.int32)])
    first_row = jnp.roll(first_row, jax.random.randint(jax.random.fold_in(key, 33), (), 0, used_count))
    second_row = jnp.roll(second_row, jax.random.randint(jax.random.fold_in(key, 34), (), 0, used_count))
    return jnp.stack([first_row, second_row]).astype(jnp.int32)


def shard_levels(key, dims, cuts, smallest, largest):
    gain = 1.0
    for axis_at, shards_of in cuts:
        steps = jax.random.uniform(jax.random.fold_in(jax.random.fold_in(key, 6), axis_at), (shards_of,), jnp.float32, smallest / len(cuts), largest / len(cuts))
        gain = gain * jnp.repeat(jnp.exp(steps), dims[axis_at] // shards_of).reshape((-1,) + (1,) * (len(dims) - 1 - axis_at))
    return gain


def centred(key, extent, spread, most, cuts=(), held_as=jnp.bfloat16):
    gain = shard_levels(key, extent, cuts, -0.22, 0.18) if cuts else 1.0
    result = jax.random.normal(key, extent, jnp.float32) * spread * gain
    return jnp.minimum(jnp.maximum(result, -most), most).astype(held_as)


def setup_inputs(seed: int = 0) -> dict:
    key_list = jax.random.split(jax.random.key(seed), 8)
    child_rhs = centred(key_list[0], (NRHS, 2 * S1), 1.0, 6.0, ((0, 4), (1, 32)), jnp.float32)
    parent_rhs = centred(key_list[1], (NRHS, S0), 1.0, 6.0, ((0, 4), (1, 32)), jnp.float32)
    child_inverse = draw_child_inverse(jax.random.fold_in(key_list[7], 71), 0)
    coupling = centred(key_list[3], (2 * S1, U), S1 ** -0.5, 0.0625, ((0, 32),))
    parent_inverse = draw_parent_inverse(jax.random.fold_in(key_list[7], 71), 0)
    child_blocks = draw_child_blocks(jax.random.fold_in(key_list[7], 71), 0)
    parent_block = draw_parent_block(jax.random.fold_in(key_list[7], 71), 0)
    return {"child_rhs": child_rhs, "parent_rhs": parent_rhs, "child_inverse": child_inverse, "coupling": coupling, "parent_inverse": parent_inverse, "child_blocks": child_blocks, "parent_block": parent_block}


def reference(child_rhs, parent_rhs, child_inverse, coupling, parent_inverse, child_blocks, parent_block):
    panels = child_rhs.astype(jnp.bfloat16)
    row_index = jnp.arange(S1, dtype=jnp.int32)
    solutions = []
    parent_total = parent_rhs.reshape(NRHS, S0 // BLK, BLK)
    for which_child in range(2):
        inverse = child_inverse[which_child * S1:(which_child + 1) * S1]
        product = jnp.dot(panels[:, which_child * S1:(which_child + 1) * S1], inverse.T, preferred_element_type=jnp.float32)
        alive_rows = row_index < BLK * child_blocks[which_child]
        solved = jnp.where(alive_rows[None, :], product, jnp.zeros_like(product))
        solutions.append(solved)
        update = jnp.dot(solved.astype(jnp.bfloat16), coupling[which_child * S1:(which_child + 1) * S1], preferred_element_type=jnp.float32)
        parent_total = parent_total.at[:, parent_block[which_child]].add(-update.reshape(NRHS, U // BLK, BLK))
    child_solution = jnp.concatenate(solutions, axis=1)
    parent_panel = parent_total.reshape(NRHS, S0).astype(jnp.bfloat16)
    parent_solution = jnp.dot(parent_panel, parent_inverse.T, preferred_element_type=jnp.float32)
    return child_solution, parent_solution
```

```python
import functools

import jax
import jax.numpy as jnp
from jax import lax
from jax.experimental import pallas as pl
from jax.experimental.pallas import tpu as pltpu
from jax.sharding import PartitionSpec as P

BLK = 128
BF = jnp.bfloat16
F32 = jnp.float32
VMEM_LIMIT = 48 * 1024 * 1024


def flat(z, x, c):
    return (z % 4) * 8 + (x % 4) * 2 + c


def receive(value, source):
    pairs = []
    for z in range(4):
        for x in range(4):
            for c in range(2):
                pairs.append((flat(*source(z, x, c)), flat(z, x, c)))
    return lax.ppermute(value, "wide", pairs)


def from_sibling(value):
    return receive(value, lambda z, x, c: (z, x, 1 - c))


STEPS = (1, -1, 2)
REL = (0, 1, -1, 2)


def along(step, first):
    def source(z, x, c):
        return (z, x + step, c) if (c == 0) == first else (z + step, x, c)

    return source


def child_part_kernel(where_ref, inv_ref, own_ref, sib_ref, acc_ref, out_ref):
    @pl.when(pl.program_id(0) == 0)
    def _():
        out_ref[...] = acc_ref[...]

    block = jnp.concatenate([own_ref[...], sib_ref[...]], axis=1)
    out_ref[...] += jnp.dot(inv_ref[...], block, preferred_element_type=F32)


def child_part_first_kernel(where_ref, inv_ref, own_ref, sib_ref, out_ref):
    block = jnp.concatenate([own_ref[...], sib_ref[...]], axis=1)
    part = jnp.dot(inv_ref[...], block, preferred_element_type=F32)

    @pl.when(pl.program_id(0) == 0)
    def _():
        out_ref[...] = part

    @pl.when(pl.program_id(0) > 0)
    def _():
        out_ref[...] += part


def child_part(where, inverse, own, sib, acc=None):
    rows, depth = inverse.shape[0], 2 * inverse.shape[0]
    steps = own.shape[0] // depth
    half = own.shape[1]
    specs = [
        pl.BlockSpec((rows, depth), lambda i, w: (0, w[i])),
        pl.BlockSpec((depth, half), lambda i, w: (i, 0)),
        pl.BlockSpec((depth, half), lambda i, w: (i, 0)),
    ]
    operands = [where, inverse, own, sib]
    kernel = child_part_first_kernel
    if acc is not None:
        specs.append(pl.BlockSpec((rows, 2 * half), lambda i, w: (0, 0)))
        operands.append(acc)
        kernel = child_part_kernel
    return pl.pallas_call(
        kernel,
        grid_spec=pltpu.PrefetchScalarGridSpec(
            num_scalar_prefetch=1,
            grid=(steps,),
            in_specs=specs,
            out_specs=pl.BlockSpec((rows, 2 * half), lambda i, w: (0, 0)),
        ),
        out_shape=jax.ShapeDtypeStruct((rows, 2 * half), F32),
        compiler_params=pltpu.CompilerParams(vmem_limit_bytes=VMEM_LIMIT),
        cost_estimate=pl.CostEstimate(
            flops=2 * rows * depth * steps * 2 * half,
            bytes_accessed=2 * rows * depth * steps,
            transcendentals=0,
        ),
    )(*operands)


def coupling_kernel(solved_ref, coupling_ref, own_ref, sib_ref):
    half = own_ref.shape[1]
    update = jnp.dot(solved_ref[...], coupling_ref[...], preferred_element_type=F32)
    own_ref[0] = update[:half]
    sib_ref[0] = update[half:].astype(BF)


def coupling_product(solved, coupling, pieces):
    columns, depth = solved.shape
    width = coupling.shape[1] // pieces
    half = columns // 2
    return pl.pallas_call(
        coupling_kernel,
        grid=(pieces,),
        in_specs=[
            pl.BlockSpec((columns, depth), lambda i: (0, 0)),
            pl.BlockSpec((depth, width), lambda i: (0, i)),
        ],
        out_specs=[
            pl.BlockSpec((1, half, width), lambda i: (i, 0, 0)),
            pl.BlockSpec((1, half, width), lambda i: (i, 0, 0)),
        ],
        out_shape=[
            jax.ShapeDtypeStruct((pieces, half, width), F32),
            jax.ShapeDtypeStruct((pieces, half, width), BF),
        ],
        compiler_params=pltpu.CompilerParams(vmem_limit_bytes=VMEM_LIMIT),
        cost_estimate=pl.CostEstimate(
            flops=2 * columns * depth * width * pieces,
            bytes_accessed=2 * depth * width * pieces,
            transcendentals=0,
        ),
    )(solved, coupling)


def pick_kernel(count, blocks_ref, p_ref, out_ref, sems):
    def copy(i):
        source = pl.ds(pl.multiple_of(blocks_ref[i] * BLK, BLK), BLK)
        return pltpu.make_async_copy(
            p_ref.at[:, source], out_ref.at[:, pl.ds(i * BLK, BLK)], sems.at[i]
        )

    for i in range(count):
        copy(i).start()
    for i in range(count):
        copy(i).wait()


def pick_columns(blocks, inverse):
    count, rows = blocks.shape[0], inverse.shape[0]
    return pl.pallas_call(
        functools.partial(pick_kernel, count),
        in_specs=[
            pl.BlockSpec(memory_space=pltpu.SMEM),
            pl.BlockSpec(memory_space=pl.ANY),
        ],
        out_specs=pl.BlockSpec(memory_space=pl.ANY),
        out_shape=jax.ShapeDtypeStruct((rows, count * BLK), inverse.dtype),
        scratch_shapes=[pltpu.SemaphoreType.DMA((count,))],
        cost_estimate=pl.CostEstimate(
            flops=0, bytes_accessed=4 * rows * count * BLK, transcendentals=0
        ),
    )(blocks, inverse)


NT = (((1,), (1,)), ((), ()))


def base_kernel(where_ref, p_ref, *refs):
    r_refs, out_ref = refs[:-1], refs[-1]
    i = pl.program_id(0)

    @pl.when(i == 0)
    def _():
        out_ref[...] = jnp.zeros_like(out_ref)

    for k, r_ref in enumerate(r_refs):

        @pl.when(i // 4 == k)
        def _(r_ref=r_ref):
            out_ref[...] += lax.dot_general(
                r_ref[i % 4], p_ref[...], NT, preferred_element_type=F32
            )


def base_product(where, inverse, parts):
    columns, rows = parts[0].shape[1:]
    steps = 4 * len(parts)
    whole = pl.BlockSpec(parts[0].shape, lambda i, w: (0, 0, 0))
    return pl.pallas_call(
        base_kernel,
        grid_spec=pltpu.PrefetchScalarGridSpec(
            num_scalar_prefetch=1,
            grid=(steps,),
            in_specs=[pl.BlockSpec((rows, rows), lambda i, w: (0, w[i]))]
            + [whole] * len(parts),
            out_specs=pl.BlockSpec((columns, rows), lambda i, w: (0, 0)),
        ),
        out_shape=jax.ShapeDtypeStruct((columns, rows), F32),
        compiler_params=pltpu.CompilerParams(vmem_limit_bytes=VMEM_LIMIT),
        cost_estimate=pl.CostEstimate(
            flops=2 * columns * rows * rows * steps,
            bytes_accessed=2 * rows * rows * steps,
            transcendentals=0,
        ),
    )(where, inverse, *parts)


def final_kernel(core_ref, base_ref, p_ref, *refs):
    own_refs, sib_refs, out_ref = refs[:4], refs[4:8], refs[8]
    half, width = own_refs[0].shape[1:]
    total = jnp.zeros(base_ref.shape, F32)
    for j in range(4):
        for i in range(4):
            block = jnp.concatenate([own_refs[j][i], sib_refs[i][j]], axis=0)
            at = (j * 4 + i) * width
            total += lax.dot_general(
                block, p_ref[:, at : at + width], NT, preferred_element_type=F32
            )
    core = core_ref[0]

    @pl.when(core == 0)
    def _():
        out_ref[...] = base_ref[...] - total

    @pl.when(core == 1)
    def _():
        out_ref[:half] = base_ref[:half] - total[half:]
        out_ref[half:] = base_ref[half:] - total[:half]


def final_product(core, base, picked, own, sib):
    vmem = pl.BlockSpec(memory_space=pltpu.VMEM)
    return pl.pallas_call(
        final_kernel,
        in_specs=[pl.BlockSpec(memory_space=pltpu.SMEM)] + [vmem] * 10,
        out_specs=vmem,
        out_shape=jax.ShapeDtypeStruct(base.shape, F32),
        compiler_params=pltpu.CompilerParams(vmem_limit_bytes=VMEM_LIMIT),
        cost_estimate=pl.CostEstimate(
            flops=2 * base.shape[0] * picked.shape[0] * picked.shape[1],
            bytes_accessed=2 * picked.shape[0] * picked.shape[1],
            transcendentals=0,
        ),
    )(core, base, picked, *own, *sib)


def gather_16(block):
    first = [block] + [receive(block, along(s, True)) for s in STEPS]
    part = jnp.stack(first)
    return [part] + [receive(part, along(s, False)) for s in STEPS]


def on_device(
    child_rhs, parent_rhs, child_inverse, coupling, parent_inverse, child_blocks, parent_block
):
    rank = lax.axis_index("wide")
    z, x, core = rank // 8, rank // 2 % 4, rank % 2
    child = z // 2
    local_rows = child_inverse.shape[0]
    columns = child_rhs.shape[0]
    half = columns // 2

    mine = child_rhs.T.astype(BF)
    keep = lax.dynamic_slice_in_dim(mine, core * half, half, axis=1)
    give = lax.dynamic_slice_in_dim(mine, (1 - core) * half, half, axis=1)
    got = from_sibling(give)
    b0 = jnp.where(
        core == 0, jnp.concatenate([keep, got], axis=0), jnp.concatenate([got, keep], axis=0)
    )
    xp = receive(b0, lambda z, x, c: (z, x + 1, c))
    xm = receive(b0, lambda z, x, c: (z, x - 1, c))
    zb = receive(b0, lambda z, x, c: (z ^ 1, x, c))
    x2 = receive(xp, lambda z, x, c: (z, x + 1, c))
    zm = receive(zb, lambda z, x, c: (z, x - 1, c))
    zp = receive(xp, lambda z, x, c: (z ^ 1, x, c))
    third = b0.shape[0] // 3
    z2 = jnp.concatenate(
        [
            receive(zp[:third], lambda z, x, c: (z, x + 1, c)),
            receive(zm[third : 2 * third], lambda z, x, c: (z, x - 1, c)),
            receive(x2[2 * third :], lambda z, x, c: (z ^ 1, x, c)),
        ],
        axis=0,
    )
    zr = z % 2
    other = 1 - zr

    def chip(zz, xx):
        return zz * 4 + xx % 4

    g1 = jnp.concatenate([b0, xp, xm, zb], axis=0)
    g2 = jnp.concatenate([x2, zm, zp], axis=0)
    w1 = jnp.stack([chip(zr, x), chip(zr, x + 1), chip(zr, x + 3), chip(other, x)])
    w2 = jnp.stack([chip(zr, x + 2), chip(other, x + 3), chip(other, x + 1)])
    w3 = jnp.stack([chip(other, x + 2)])
    acc = child_part(w1, child_inverse, g1, from_sibling(g1))
    acc = child_part(w2, child_inverse, g2, from_sibling(g2), acc)
    acc = child_part(w3, child_inverse, z2, from_sibling(z2), acc)

    row = (rank % 16) * local_rows + jnp.arange(local_rows, dtype=jnp.int32)
    limit = BLK * jnp.take(child_blocks, child)
    solved = jnp.where((row < limit)[:, None], acc, jnp.zeros_like(acc))
    swapped = jnp.concatenate([solved[:, half:], solved[:, :half]], axis=1)
    child_solution = jnp.where(core == 0, solved, swapped).T

    own, sib = coupling_product(solved.T.astype(BF), coupling, 8)
    chip_sum = (own + from_sibling(sib).astype(F32)).astype(BF)
    groups = [
        [flat(2 * h + dz, xx, c) for dz in range(2) for xx in range(4)]
        for h in range(2)
        for c in range(2)
    ]
    pieces = lax.all_to_all(
        chip_sum, "wide", split_axis=0, concat_axis=0, axis_index_groups=groups, tiled=True
    )
    update = jnp.sum(pieces.astype(F32), axis=0).astype(BF)
    u_own = gather_16(update)
    u_sib = [from_sibling(part) for part in u_own]

    r_own = gather_16(parent_rhs.astype(BF))
    r_sib = [from_sibling(part) for part in r_own]

    def places(c):
        rel = jnp.array(REL, jnp.int32)
        second, first = rel[:, None], rel[None, :]
        dx = jnp.where(c == 0, first, second)
        dz = jnp.where(c == 0, second, first)
        return ((z + dz) % 4).reshape(-1), ((x + dx) % 4).reshape(-1)

    zs, xs = places(core)
    zs_sib, xs_sib = places(1 - core)
    where = jnp.concatenate(
        [zs * 8 + xs * 2 + core, zs_sib * 8 + xs_sib * 2 + (1 - core)]
    )
    base = base_product(where, parent_inverse, r_own + r_sib)
    table = parent_block.reshape(2 * 8, 3)
    blocks = table[zs * 4 + xs].reshape(-1)
    picked = pick_columns(blocks, parent_inverse)
    parent_solution = final_product(core.reshape(1), base, picked, u_own, u_sib)
    return (child_solution, parent_solution)


def solution(mesh):
    placed = (
        P("rhs", "wide"),
        P("rhs", "wide"),
        P("wide", None),
        P("wide", None),
        P("wide", None),
        P(),
        P(),
    )
    return jax.shard_map(
        on_device,
        mesh=mesh,
        in_specs=placed,
        out_specs=(P("rhs", "wide"), P("rhs", "wide")),
        check_vma=False,
    )
```

```python
import functools

import jax
import jax.numpy as jnp
from jax import lax
from jax.experimental import pallas as pl
from jax.experimental.pallas import tpu as pltpu
from jax.sharding import PartitionSpec as P

BLK = 128
BF = jnp.bfloat16
F32 = jnp.float32
BANDS = 8
VMEM_LIMIT = 12 * 1024 * 1024


def flat(z, x, c):
    return (z % 4) * 8 + (x % 4) * 2 + c


def receive(value, source):
    pairs = []
    for z in range(4):
        for x in range(4):
            for c in range(2):
                pairs.append((flat(*source(z, x, c)), flat(z, x, c)))
    return lax.ppermute(value, "wide", pairs)


def from_sibling(value):
    return receive(value, lambda z, x, c: (z, x, 1 - c))


def tie(*values):
    return lax.optimization_barrier(values)


STEPS = (1, -1, 2)
REL = (0, 1, -1, 2)


def along(step, first):
    def source(z, x, c):
        return (z, x + step, c) if (c == 0) == first else (z + step, x, c)

    return source


VMEM = pl.BlockSpec(memory_space=pltpu.VMEM)
SMEM = pl.BlockSpec(memory_space=pltpu.SMEM)


HBM = pl.BlockSpec(memory_space=pltpu.HBM)


def call(kernel, out_shape, flops, nbytes, *operands, smem=0, hbm=(), scratch=()):
    specs = [SMEM if i < smem else HBM if i in hbm else VMEM for i in range(len(operands))]
    operands = [
        pltpu.with_memory_space_constraint(operand, pltpu.HBM) if i in hbm else operand
        for i, operand in enumerate(operands)
    ]
    return pl.pallas_call(
        kernel,
        in_specs=specs,
        out_specs=jax.tree.map(lambda _: VMEM, out_shape),
        out_shape=out_shape,
        scratch_shapes=scratch,
        compiler_params=pltpu.CompilerParams(vmem_limit_bytes=VMEM_LIMIT),
        cost_estimate=pl.CostEstimate(flops=flops, bytes_accessed=nbytes, transcendentals=0),
    )(*operands)


def shape(dims, dtype):
    return jax.ShapeDtypeStruct(dims, dtype)


def load_kernel(count, sources, *refs):
    targets, sems = refs[:count], refs[count]
    copies = []
    for k in range(count):
        band = sources[k].shape[0] // BANDS
        for i in range(BANDS):
            rows = pl.ds(i * band, band)
            copies.append(
                pltpu.make_async_copy(sources[k].at[rows], targets[k].at[rows], sems.at[k, i])
            )
    for copy in copies:
        copy.start()
    for copy in copies:
        copy.wait()


def load(*arrays):
    count = len(arrays)

    def kernel(*refs):
        load_kernel(count, refs[:count], *refs[count:])

    return call(
        kernel,
        [shape(a.shape, a.dtype) for a in arrays],
        0,
        sum(2 * a.size for a in arrays),
        *arrays,
        hbm=range(count),
        scratch=[pltpu.SemaphoreType.DMA((count, BANDS))],
    )


def place():
    rank = lax.axis_index("wide")
    return rank // 8, rank // 2 % 4, rank % 2


def part_sum(chips, inv_ref, own_ref, sib_ref, total):
    depth = 2 * inv_ref.shape[0]
    z, x, _ = place()
    for i, (dz, dx) in enumerate(chips):
        rows = slice(i * depth, (i + 1) * depth)
        block = jnp.concatenate([own_ref[rows], sib_ref[rows]], axis=1)
        at = ((z + dz) % 2 * 4 + (x + dx) % 4) * depth
        columns = pl.ds(pl.multiple_of(at, BLK), depth)
        part = jnp.dot(inv_ref[:, columns], block, preferred_element_type=F32)
        total = part if total is None else total + part
    return total


def child_part(chips, inverse, own, sib, *acc):
    rows, columns = inverse.shape[0], 2 * own.shape[1]

    def kernel(inv_ref, own_ref, sib_ref, *refs):
        acc = refs[0][...] if len(refs) > 1 else None
        refs[-1][...] = part_sum(chips, inv_ref, own_ref, sib_ref, acc)

    return call(
        kernel,
        shape((rows, columns), F32),
        2 * rows * own.shape[0] * columns,
        2 * rows * own.shape[0],
        inverse,
        own,
        sib,
        *acc,
    )


def child_last_kernel(
    chips, blocks_ref, inv_ref, own_ref, sib_ref, acc_ref, coupling_ref, out_ref, keep_ref, give_ref
):
    total = part_sum(chips, inv_ref, own_ref, sib_ref, acc_ref[...])
    half = own_ref.shape[1]
    z, x, core = place()
    row = lax.broadcasted_iota(jnp.int32, total.shape, 0)
    first = (z % 2 * 8 + x * 2 + core) * total.shape[0]
    limit = BLK * blocks_ref[z // 2] - first
    total = jnp.where(row < limit, total, 0.0)

    @pl.when(core == 0)
    def _():
        out_ref[...] = total

    @pl.when(core == 1)
    def _():
        out_ref[:, :half] = total[:, half:]
        out_ref[:, half:] = total[:, :half]

    solved = total.T.astype(BF)
    pieces, _, width = keep_ref.shape
    for i in range(pieces):
        update = jnp.dot(
            solved, coupling_ref[:, i * width : (i + 1) * width], preferred_element_type=F32
        )
        keep_ref[i] = update[:half]
        give_ref[i] = update[half:].astype(BF)


def child_last(chips, blocks, inverse, own, sib, acc, coupling, pieces):
    rows, columns = acc.shape
    half, width = columns // 2, coupling.shape[1] // pieces
    return call(
        functools.partial(child_last_kernel, chips),
        [
            shape((rows, columns), F32),
            shape((pieces, half, width), F32),
            shape((pieces, half, width), BF),
        ],
        2 * columns * rows * (own.shape[0] + coupling.shape[1]),
        2 * rows * (own.shape[0] + coupling.shape[1]),
        blocks,
        inverse,
        own,
        sib,
        acc,
        coupling,
        smem=1,
    )


def pack_kernel(x2_ref, zm_ref, zp_ref, group_ref, a_ref, b_ref, c_ref):
    rows = x2_ref.shape[0]
    third = rows // 3
    group_ref[:rows] = x2_ref[...]
    group_ref[rows : 2 * rows] = zm_ref[...]
    group_ref[2 * rows :] = zp_ref[...]
    a_ref[...] = zp_ref[:third]
    b_ref[...] = zm_ref[third : 2 * third]
    c_ref[...] = x2_ref[2 * third :]


def pack(x2, zm, zp):
    rows, half = x2.shape
    return call(
        pack_kernel,
        [shape((3 * rows, half), BF)] + [shape((rows // 3, half), BF)] * 3,
        0,
        16 * rows * half,
        x2,
        zm,
        zp,
    )


def reduce_kernel(pieces_ref, out_ref):
    total = pieces_ref[0].astype(F32)
    for i in range(1, pieces_ref.shape[0]):
        total += pieces_ref[i].astype(F32)
    out_ref[...] = total.T.astype(BF)


def reduce_pieces(pieces):
    count, half, width = pieces.shape
    return call(reduce_kernel, shape((width, half), BF), 0, 4 * count * half * width, pieces)


def chip_at(i, j, core):
    z, x, _ = place()
    dx = jnp.where(core == 0, REL[i], REL[j])
    dz = jnp.where(core == 0, REL[j], REL[i])
    return (z + dz + 4) % 4, (x + dx + 4) % 4


def base_kernel(blocks_ref, p_ref, *refs):
    r_refs, (out_ref, picked_ref) = refs[:-2], refs[-2:]
    rows = p_ref.shape[0]
    core = place()[2]
    total = None
    for k, r_ref in enumerate(r_refs):
        owner = core if k < 4 else 1 - core
        for i in range(4):
            z, x = chip_at(i, k % 4, owner)
            at = pl.multiple_of((z * 8 + x * 2 + owner) * rows, BLK)
            part = jnp.dot(p_ref[:, pl.ds(at, rows)], r_ref[i], preferred_element_type=F32)
            total = part if total is None else total + part
    out_ref[...] = total
    for n in range(picked_ref.shape[1] // BLK):
        z, x = chip_at(n // 3 % 4, n // 12, core)
        block = blocks_ref[z // 2, (z % 2 * 4 + x) * 3 + n % 3]
        at = pl.multiple_of(block * BLK, BLK)
        picked_ref[:, n * BLK : (n + 1) * BLK] = p_ref[:, pl.ds(at, BLK)]


def base_product(blocks, inverse, parts):
    rows, order = inverse.shape
    columns = parts[0].shape[2]
    return call(
        base_kernel,
        [shape((rows, columns), F32), shape((rows, blocks.size * BLK), inverse.dtype)],
        2 * rows * order * columns,
        2 * rows * order,
        blocks,
        inverse,
        *parts,
        smem=1,
    )


def final_kernel(base_ref, p_ref, *refs):
    own_refs, sib_refs, out_ref = refs[:4], refs[4:8], refs[8]
    width, half = own_refs[0].shape[1:]
    total = base_ref[...]
    change = None
    for j in range(4):
        for i in range(4):
            block = jnp.concatenate([own_refs[j][i], sib_refs[i][j]], axis=1)
            at = (j * 4 + i) * width
            part = jnp.dot(p_ref[:, at : at + width], block, preferred_element_type=F32)
            change = part if change is None else change + part
    core = place()[2]

    @pl.when(core == 0)
    def _():
        out_ref[...] = (total - change).T

    @pl.when(core == 1)
    def _():
        out_ref[:half] = (total[:, :half] - change[:, half:]).T
        out_ref[half:] = (total[:, half:] - change[:, :half]).T


def final_product(base, picked, own, sib):
    rows, columns = base.shape
    return call(
        final_kernel,
        shape((columns, rows), F32),
        2 * columns * picked.shape[0] * picked.shape[1],
        2 * picked.shape[0] * picked.shape[1],
        base,
        picked,
        *own,
        *sib,
    )


def gather_first(block):
    return [block] + [receive(block, along(s, True)) for s in STEPS]


def gather_second(first):
    part = jnp.stack(first)
    return [part] + [receive(part, along(s, False)) for s in STEPS]


def on_device(
    child_rhs, parent_rhs, child_inverse, coupling, parent_inverse, child_blocks, parent_block
):
    core = lax.axis_index("wide") % 2
    half = child_rhs.shape[0] // 2

    mine = child_rhs.T.astype(BF)
    keep = lax.dynamic_slice_in_dim(mine, core * half, half, axis=1)
    give = lax.dynamic_slice_in_dim(mine, (1 - core) * half, half, axis=1)
    got = from_sibling(give)
    b0 = jnp.where(
        core == 0, jnp.concatenate([keep, got], axis=0), jnp.concatenate([got, keep], axis=0)
    )
    xp = receive(b0, lambda z, x, c: (z, x + 1, c))
    xm = receive(b0, lambda z, x, c: (z, x - 1, c))
    zb = receive(b0, lambda z, x, c: (z ^ 1, x, c))
    r_first = gather_first(parent_rhs.T.astype(BF))
    (child_inverse,) = load(child_inverse)
    xp, xm, zb, child_inverse, *r_first = tie(xp, xm, zb, child_inverse, *r_first)
    g1 = jnp.concatenate([b0, xp, xm, zb], axis=0)
    g1_sib = from_sibling(g1)
    x2 = receive(xp, lambda z, x, c: (z, x + 1, c))
    zm = receive(zb, lambda z, x, c: (z, x - 1, c))
    zp = receive(xp, lambda z, x, c: (z ^ 1, x, c))
    coupling, parent_inverse = load(coupling, parent_inverse)
    r_own = gather_second(r_first)
    acc = child_part([(0, 0), (0, 1), (0, 3), (1, 0)], child_inverse, g1, g1_sib)
    x2, zm, zp, acc, coupling, parent_inverse, *r_own[1:3] = tie(
        x2, zm, zp, acc, coupling, parent_inverse, *r_own[1:3]
    )
    g2, last_a, last_b, last_c = pack(x2, zm, zp)
    z2 = jnp.concatenate(
        [
            receive(last_a, lambda z, x, c: (z, x + 1, c)),
            receive(last_b, lambda z, x, c: (z, x - 1, c)),
            receive(last_c, lambda z, x, c: (z ^ 1, x, c)),
        ],
        axis=0,
    )
    acc = child_part([(0, 2), (1, 3), (1, 1)], child_inverse, g2, from_sibling(g2), acc)
    z2, acc = tie(z2, acc)
    solution_t, keep, give = child_last(
        [(1, 2)], child_blocks, child_inverse, z2, from_sibling(z2), acc, coupling, 8
    )

    chip_sum = (keep + from_sibling(give).astype(F32)).astype(BF)
    groups = [
        [flat(2 * h + dz, xx, c) for dz in range(2) for xx in range(4)]
        for h in range(2)
        for c in range(2)
    ]
    chip_sum, r_own[3] = tie(chip_sum, r_own[3])
    pieces = lax.all_to_all(
        chip_sum, "wide", split_axis=0, concat_axis=0, axis_index_groups=groups, tiled=True
    )
    r_sib = [from_sibling(part) for part in r_own]
    base, picked = base_product(parent_block, parent_inverse, r_own + r_sib)
    update, base, picked = tie(reduce_pieces(pieces), base, picked)
    u_own = gather_second(gather_first(update))
    u_sib = [from_sibling(part) for part in u_own]
    parent_solution = final_product(base, picked, u_own, u_sib)
    return (solution_t.T, parent_solution)


def solution(mesh):
    placed = (
        P("rhs", "wide"),
        P("rhs", "wide"),
        P("wide", None),
        P("wide", None),
        P("wide", None),
        P(),
        P(),
    )
    return jax.shard_map(
        on_device,
        mesh=mesh,
        in_specs=placed,
        out_specs=(P("rhs", "wide"), P("rhs", "wide")),
        check_vma=False,
    )
```

```python
import functools

import jax
import jax.numpy as jnp
from jax import lax
from jax.experimental import pallas as pl
from jax.experimental.pallas import tpu as pltpu
from jax.sharding import PartitionSpec as P

BLK = 128
BF = jnp.bfloat16
F32 = jnp.float32
BANDS = 8
VMEM_LIMIT = 8 * 1024 * 1024


def flat(z, x, c):
    return (z % 4) * 8 + (x % 4) * 2 + c


def receive(value, source):
    pairs = []
    for z in range(4):
        for x in range(4):
            for c in range(2):
                pairs.append((flat(*source(z, x, c)), flat(z, x, c)))
    return lax.ppermute(value, "wide", pairs)


def from_sibling(value):
    return receive(value, lambda z, x, c: (z, x, 1 - c))


def tie(*values):
    return lax.optimization_barrier(values)


STEPS = (1, -1, 2)
REL = (0, 1, -1, 2)


def along(step, first):
    def source(z, x, c):
        return (z, x + step, c) if (c == 0) == first else (z + step, x, c)

    return source


VMEM = pl.BlockSpec(memory_space=pltpu.VMEM)
SMEM = pl.BlockSpec(memory_space=pltpu.SMEM)


HBM = pl.BlockSpec(memory_space=pltpu.HBM)


def call(kernel, out_shape, *operands, smem=0, hbm=(), scratch=()):
    specs = [SMEM if i < smem else HBM if i in hbm else VMEM for i in range(len(operands))]
    operands = [
        pltpu.with_memory_space_constraint(operand, pltpu.HBM) if i in hbm else operand
        for i, operand in enumerate(operands)
    ]
    return pl.pallas_call(
        kernel,
        in_specs=specs,
        out_specs=jax.tree.map(lambda _: VMEM, out_shape),
        out_shape=out_shape,
        scratch_shapes=scratch,
        compiler_params=pltpu.CompilerParams(vmem_limit_bytes=VMEM_LIMIT),
        cost_estimate=pl.CostEstimate(flops=0, bytes_accessed=0, transcendentals=0),
    )(*operands)


def shape(dims, dtype):
    return jax.ShapeDtypeStruct(dims, dtype)


def load_kernel(count, sources, *refs):
    targets, sems = refs[:count], refs[count]
    copies = []
    for k in range(count):
        band = sources[k].shape[0] // BANDS
        for i in range(BANDS):
            rows = pl.ds(i * band, band)
            copies.append(
                pltpu.make_async_copy(sources[k].at[rows], targets[k].at[rows], sems.at[k, i])
            )
    for copy in copies:
        copy.start()
    for copy in copies:
        copy.wait()


def load(*arrays):
    count = len(arrays)

    def kernel(*refs):
        load_kernel(count, refs[:count], *refs[count:])

    return call(
        kernel,
        [shape(a.shape, a.dtype) for a in arrays],
        *arrays,
        hbm=range(count),
        scratch=[pltpu.SemaphoreType.DMA((count, BANDS))],
    )


def place():
    rank = lax.axis_index("wide")
    return rank // 8, rank // 2 % 4, rank % 2


def part_sum(chips, inv_ref, block_refs, held_ref, total):
    rows = inv_ref.shape[0]
    z, x, core = place()
    mine = pl.ds(pl.multiple_of(core * rows, 16), rows)
    others = pl.ds(pl.multiple_of((1 - core) * rows, 16), rows)
    for i, (dz, dx) in enumerate(chips):
        held_ref[i, mine] = block_refs[i][...]
        held_ref[i, others] = block_refs[len(chips) + i][...]
        at = ((z + dz) % 2 * 4 + (x + dx) % 4) * 2 * rows
        columns = pl.ds(pl.multiple_of(at, BLK), 2 * rows)
        part = jnp.dot(inv_ref[:, columns], held_ref[i], preferred_element_type=F32)
        total = part if total is None else total + part
    return total


def held_scratch(chips, inverse, columns):
    return pltpu.VMEM((len(chips), 2 * inverse.shape[0], columns), BF)


def child_part(chips, inverse, blocks, *acc):
    rows, columns = blocks[0].shape
    count = len(blocks)

    def kernel(inv_ref, *refs):
        block_refs, refs = refs[:count], refs[count:]
        start = refs[0][...] if acc else None
        out_ref, held_ref = refs[-2:]
        out_ref[...] = part_sum(chips, inv_ref, block_refs, held_ref, start)

    return call(
        kernel,
        shape((rows, columns), F32),
        inverse,
        *blocks,
        *acc,
        scratch=[held_scratch(chips, inverse, columns)],
    )


def child_last(chips, blocks, acc, inverse, coupling, child_blocks, pieces):
    rows, columns = acc.shape
    half, width = columns // 2, coupling.shape[1] // pieces
    count = len(blocks)

    def kernel(sizes_ref, inv_ref, coupling_ref, acc_ref, *refs):
        block_refs, refs = refs[:count], refs[count:]
        out_ref, keep_ref, *give_refs, held_ref, solved_ref = refs
        total = part_sum(chips, inv_ref, block_refs, held_ref, acc_ref[...])
        z, x, core = place()
        row = lax.broadcasted_iota(jnp.int32, total.shape, 0)
        first = (z % 2 * 8 + x * 2 + core) * rows
        limit = BLK * sizes_ref[z // 2] - first
        total = jnp.where(row < limit, total, 0.0)
        out_ref[...] = total
        solved_ref[...] = total.T.astype(BF)
        mine = pl.ds(pl.multiple_of(core * half, half), half)
        others = pl.ds(pl.multiple_of((1 - core) * half, half), half)
        solved = jnp.concatenate([solved_ref[mine], solved_ref[others]], axis=0)
        for i in range(pieces):
            update = jnp.dot(
                solved, coupling_ref[:, i * width : (i + 1) * width], preferred_element_type=F32
            )
            keep_ref[i] = update[:half]
            give_refs[2 * i // pieces][i % (pieces // 2)] = update[half:].astype(BF)

    return call(
        kernel,
        [
            shape((rows, columns), F32),
            shape((pieces, half, width), F32),
        ]
        + [shape((pieces // 2, half, width), BF)] * 2,
        child_blocks,
        inverse,
        coupling,
        acc,
        *blocks,
        smem=1,
        scratch=[held_scratch(chips, inverse, columns), pltpu.VMEM((columns, rows), BF)],
    )


def thirds(zp, zm, x2):
    rows, columns = x2.shape
    third = rows // 3

    def kernel(zp_ref, zm_ref, x2_ref, *out_refs):
        for i, ref in enumerate((zp_ref, zm_ref, x2_ref)):
            out_refs[i][...] = ref[i * third : (i + 1) * third]

    return call(kernel, [shape((third, columns), BF)] * 3, zp, zm, x2)


def reduce_kernel(pieces_ref, out_ref):
    total = pieces_ref[0].astype(F32)
    for i in range(1, pieces_ref.shape[0]):
        total += pieces_ref[i].astype(F32)
    out_ref[...] = total.T.astype(BF)


def reduce_pieces(pieces):
    count, half, width = pieces.shape
    return call(reduce_kernel, shape((width, half), BF), pieces)


def chip_at(i, j, core):
    z, x, _ = place()
    dx = jnp.where(core == 0, REL[i], REL[j])
    dz = jnp.where(core == 0, REL[j], REL[i])
    return (z + dz + 4) % 4, (x + dx + 4) % 4


def base_kernel(blocks_ref, p_ref, *refs):
    r_refs, (out_ref, picked_ref) = refs[:-2], refs[-2:]
    rows = p_ref.shape[0]
    core = place()[2]
    total = None
    for k, r_ref in enumerate(r_refs):
        owner = core if k < len(ENTRIES) else 1 - core
        for n, (i, j) in enumerate(ENTRIES[k % len(ENTRIES)]):
            z, x = chip_at(i, j, owner)
            at = pl.multiple_of((z * 8 + x * 2 + owner) * rows, BLK)
            part = jnp.dot(p_ref[:, pl.ds(at, rows)], r_ref[n], preferred_element_type=F32)
            total = part if total is None else total + part
    out_ref[...] = total
    for n in range(picked_ref.shape[1] // BLK):
        z, x = chip_at(n // 3 % 4, n // 12, core)
        block = blocks_ref[z // 2, (z % 2 * 4 + x) * 3 + n % 3]
        at = pl.multiple_of(block * BLK, BLK)
        picked_ref[:, n * BLK : (n + 1) * BLK] = p_ref[:, pl.ds(at, BLK)]


def base_product(blocks, inverse, parts):
    rows, order = inverse.shape
    columns = parts[0].shape[2]
    return call(
        base_kernel,
        [shape((rows, columns), F32), shape((rows, blocks.size * BLK), inverse.dtype)],
        blocks,
        inverse,
        *parts,
        smem=1,
    )


def final_kernel(base_ref, p_ref, *refs):
    own_refs, sib_refs, out_ref = refs[:4], refs[4:8], refs[8]
    width, half = own_refs[0].shape[1:]
    total = base_ref[...]
    change = None
    for j in range(4):
        for i in range(4):
            block = jnp.concatenate([own_refs[j][i], sib_refs[i][j]], axis=1)
            at = (j * 4 + i) * width
            part = jnp.dot(p_ref[:, at : at + width], block, preferred_element_type=F32)
            change = part if change is None else change + part
    core = place()[2]

    @pl.when(core == 0)
    def _():
        out_ref[...] = (total - change).T

    @pl.when(core == 1)
    def _():
        out_ref[:half] = (total[:, :half] - change[:, half:]).T
        out_ref[half:] = (total[:, half:] - change[:, :half]).T


def final_product(base, picked, own, sib):
    rows, columns = base.shape
    return call(
        final_kernel,
        shape((columns, rows), F32),
        base,
        picked,
        *own,
        *sib,
    )


def gather_first(block):
    return [block] + [receive(block, along(s, True)) for s in STEPS]


def gather_second(first, far=True):
    part = jnp.stack(first)
    return [part] + [receive(part, along(s, False)) for s in STEPS[: 3 if far else 2]]


def halves(up, down):
    count = up.shape[0] // 2
    cut = shape((count,) + up.shape[1:], up.dtype)

    def kernel(up_ref, down_ref, a_ref, b_ref):
        a_ref[...] = up_ref[:count]
        b_ref[...] = down_ref[count:]

    return call(kernel, [cut, cut], up, down)


def gather_far(near):
    a, b = halves(near[1], near[2])
    return [receive(a, along(1, False)), receive(b, along(-1, False))]


ENTRIES = [[(i, j) for i in range(4)] for j in range(3)] + [[(0, 3), (1, 3)], [(2, 3), (3, 3)]]


def on_device(
    child_rhs, parent_rhs, child_inverse, coupling, parent_inverse, child_blocks, parent_block
):
    b0 = child_rhs.T.astype(BF)
    b0_sib = from_sibling(b0)
    xp = receive(b0, lambda z, x, c: (z, x + 1, c))
    xm = receive(b0, lambda z, x, c: (z, x - 1, c))
    zb = receive(b0, lambda z, x, c: (z ^ 1, x, c))
    child_inverse, coupling = load(child_inverse, coupling)
    root = parent_rhs.T.astype(BF)
    xp, xm, zb, b0_sib, child_inverse, coupling, root = tie(
        xp, xm, zb, b0_sib, child_inverse, coupling, root
    )
    near = [b0, xp, xm, zb, b0_sib] + [from_sibling(v) for v in (xp, xm, zb)]
    acc = child_part([(0, 0), (0, 1), (0, 3), (1, 0)], child_inverse, near)
    x2 = receive(xp, lambda z, x, c: (z, x + 1, c))
    zm = receive(zb, lambda z, x, c: (z, x - 1, c))
    zp = receive(xp, lambda z, x, c: (z ^ 1, x, c))
    x2, zm, zp, acc = tie(x2, zm, zp, acc)
    last_a, last_b, last_c = thirds(zp, zm, x2)
    mid = [x2, zm, zp] + [from_sibling(v) for v in (x2, zm, zp)]
    root, mid[3] = tie(root, mid[3])
    acc = child_part([(0, 2), (1, 3), (1, 1)], child_inverse, mid, acc)
    r_near = gather_second(gather_first(root), far=False)
    z2 = jnp.concatenate(
        [
            receive(last_a, lambda z, x, c: (z, x + 1, c)),
            receive(last_b, lambda z, x, c: (z, x - 1, c)),
            receive(last_c, lambda z, x, c: (z ^ 1, x, c)),
        ],
        axis=0,
    )
    z2, acc = tie(z2, acc)
    solution_t, keep, *give = child_last(
        [(1, 2)], [z2, from_sibling(z2)], acc, child_inverse, coupling, child_blocks, 8
    )

    got = jnp.concatenate([from_sibling(part) for part in give], axis=0)
    chip_sum = (keep + got.astype(F32)).astype(BF)
    groups = [
        [flat(2 * h + dz, xx, c) for dz in range(2) for xx in range(4)]
        for h in range(2)
        for c in range(2)
    ]
    chip_sum, *r_near = tie(chip_sum, *r_near)
    pieces = lax.all_to_all(
        chip_sum, "wide", split_axis=0, concat_axis=0, axis_index_groups=groups, tiled=True
    )
    r_far = gather_far(r_near)
    r_near_sib = [from_sibling(part) for part in r_near]
    pieces, *r_near_sib = tie(pieces, *r_near_sib)
    u_first = gather_first(reduce_pieces(pieces))
    *u_first, r_far[0], r_far[1] = tie(*u_first, *r_far)
    u_own = gather_second(u_first)
    r_far_sib = [from_sibling(part) for part in r_far]
    base, picked = base_product(
        parent_block, parent_inverse, [*r_near, *r_far, *r_near_sib, *r_far_sib]
    )
    base, picked, *u_own = tie(base, picked, *u_own)
    u_sib = [from_sibling(part) for part in u_own]
    parent_solution = final_product(base, picked, u_own, u_sib)
    return (solution_t.T, parent_solution)


def solution(mesh):
    placed = (
        P("rhs", "wide"),
        P("rhs", "wide"),
        P("wide", None),
        P("wide", None),
        P("wide", None),
        P(),
        P(),
    )
    return jax.shard_map(
        on_device,
        mesh=mesh,
        in_specs=placed,
        out_specs=(P("rhs", "wide"), P("rhs", "wide")),
        check_vma=False,
    )
```

```python
import functools

import jax
import jax.numpy as jnp
from jax import lax
from jax.experimental import pallas as pl
from jax.experimental.pallas import tpu as pltpu
from jax.sharding import PartitionSpec as P

BLK = 128
BF = jnp.bfloat16
F32 = jnp.float32
BANDS = 8
VMEM_LIMIT = 8 * 1024 * 1024


def flat(z, x, c):
    return (z % 4) * 8 + (x % 4) * 2 + c


def receive(value, source):
    pairs = []
    for z in range(4):
        for x in range(4):
            for c in range(2):
                pairs.append((flat(*source(z, x, c)), flat(z, x, c)))
    return lax.ppermute(value, "wide", pairs)


def from_sibling(value):
    return receive(value, lambda z, x, c: (z, x, 1 - c))


def tie(*values):
    return lax.optimization_barrier(values)


STEPS = (1, -1, 2)
REL = (0, 1, -1, 2)


def along(step, first):
    def source(z, x, c):
        return (z, x + step, c) if (c == 0) == first else (z + step, x, c)

    return source


VMEM = pl.BlockSpec(memory_space=pltpu.VMEM)
SMEM = pl.BlockSpec(memory_space=pltpu.SMEM)


HBM = pl.BlockSpec(memory_space=pltpu.HBM)


def call(kernel, out_shape, *operands, smem=0, hbm=(), scratch=(), weight=0):
    specs = [SMEM if i < smem else HBM if i in hbm else VMEM for i in range(len(operands))]
    operands = [
        pltpu.with_memory_space_constraint(operand, pltpu.HBM) if i in hbm else operand
        for i, operand in enumerate(operands)
    ]
    return pl.pallas_call(
        kernel,
        in_specs=specs,
        out_specs=jax.tree.map(lambda _: VMEM, out_shape),
        out_shape=out_shape,
        scratch_shapes=scratch,
        compiler_params=pltpu.CompilerParams(vmem_limit_bytes=VMEM_LIMIT),
        cost_estimate=pl.CostEstimate(flops=0, bytes_accessed=weight, transcendentals=0),
    )(*operands)


def shape(dims, dtype):
    return jax.ShapeDtypeStruct(dims, dtype)


def load_kernel(count, sources, *refs):
    targets, sems = refs[:count], refs[count]
    copies = []
    for k in range(count):
        band = sources[k].shape[0] // BANDS
        for i in range(BANDS):
            rows = pl.ds(i * band, band)
            copies.append(
                pltpu.make_async_copy(sources[k].at[rows], targets[k].at[rows], sems.at[k, i])
            )
    for copy in copies:
        copy.start()
    for copy in copies:
        copy.wait()


def load(*arrays):
    count = len(arrays)

    def kernel(*refs):
        load_kernel(count, refs[:count], *refs[count:])

    return call(
        kernel,
        [shape(a.shape, a.dtype) for a in arrays],
        *arrays,
        hbm=range(count),
        scratch=[pltpu.SemaphoreType.DMA((count, BANDS))],
    )


def place():
    rank = lax.axis_index("wide")
    return rank // 8, rank // 2 % 4, rank % 2


def part_sum(chips, inv_ref, block_refs, held_ref, total):
    rows = inv_ref.shape[0]
    z, x, core = place()
    mine = pl.ds(pl.multiple_of(core * rows, 16), rows)
    others = pl.ds(pl.multiple_of((1 - core) * rows, 16), rows)
    for i, (dz, dx) in enumerate(chips):
        held_ref[i, mine] = block_refs[i]
        held_ref[i, others] = block_refs[len(chips) + i]
        at = ((z + dz) % 2 * 4 + (x + dx) % 4) * 2 * rows
        columns = pl.ds(pl.multiple_of(at, BLK), 2 * rows)
        part = jnp.dot(inv_ref[:, columns], held_ref[i], preferred_element_type=F32)
        total = part if total is None else total + part
    return total


def held_scratch(chips, inverse, columns):
    return pltpu.VMEM((len(chips), 2 * inverse.shape[0], columns), BF)


def entries(refs):
    blocks = []
    for ref in refs:
        blocks += [ref[...]] if len(ref.shape) == 2 else [ref[i] for i in range(ref.shape[0])]
    return blocks


def child_part(chips, inverse, blocks, *acc):
    rows, columns = blocks[0].shape[-2:]
    count = len(blocks)

    def kernel(inv_ref, *refs):
        block_refs, refs = refs[:count], refs[count:]
        start = refs[0][...] if acc else None
        out_ref, held_ref = refs[-2:]
        out_ref[...] = part_sum(chips, inv_ref, entries(block_refs), held_ref, start)

    return call(
        kernel,
        shape((rows, columns), F32),
        inverse,
        *blocks,
        *acc,
        scratch=[held_scratch(chips, inverse, columns)],
    )


def child_last(chips, blocks, acc, inverse, coupling, child_blocks, pieces):
    rows, columns = acc.shape
    half, width = columns // 2, coupling.shape[1] // pieces
    count = len(blocks)

    def kernel(sizes_ref, inv_ref, coupling_ref, acc_ref, *refs):
        block_refs, refs = refs[:count], refs[count:]
        out_ref, keep_ref, *give_refs, held_ref, solved_ref = refs
        total = part_sum(chips, inv_ref, entries(block_refs), held_ref, acc_ref[...])
        z, x, core = place()
        row = lax.broadcasted_iota(jnp.int32, total.shape, 0)
        first = (z % 2 * 8 + x * 2 + core) * rows
        limit = BLK * sizes_ref[z // 2] - first
        total = jnp.where(row < limit, total, 0.0)
        out_ref[...] = total
        solved_ref[...] = total.T.astype(BF)
        mine = pl.ds(pl.multiple_of(core * half, half), half)
        others = pl.ds(pl.multiple_of((1 - core) * half, half), half)
        solved = jnp.concatenate([solved_ref[mine], solved_ref[others]], axis=0)
        for i in range(pieces):
            update = jnp.dot(
                solved, coupling_ref[:, i * width : (i + 1) * width], preferred_element_type=F32
            )
            keep_ref[i] = update[:half]
            give_refs[2 * i // pieces][i % (pieces // 2)] = update[half:].astype(BF)

    return call(
        kernel,
        [
            shape((rows, columns), F32),
            shape((pieces, half, width), F32),
        ]
        + [shape((pieces // 2, half, width), BF)] * 2,
        child_blocks,
        inverse,
        coupling,
        acc,
        *blocks,
        smem=1,
        scratch=[held_scratch(chips, inverse, columns), pltpu.VMEM((columns, rows), BF)],
    )


def turn(block):
    def kernel(block_ref, out_ref):
        out_ref[...] = block_ref[...].T.astype(BF)

    return call(kernel, shape(block.shape[::-1], BF), block)


def pile(*blocks):
    def kernel(*refs):
        for i, ref in enumerate(refs[:-1]):
            refs[-1][i] = ref[...]

    return call(kernel, shape((len(blocks),) + blocks[0].shape, BF), *blocks)


def pile_and_cut(x2, zm, zp):
    rows, columns = x2.shape

    def kernel(x2_ref, zm_ref, zp_ref, pile_ref, a_ref, b_ref):
        for i, ref in enumerate((x2_ref, zm_ref, zp_ref)):
            pile_ref[i] = ref[...]
        a_ref[...] = zp_ref[: rows // 2]
        b_ref[...] = zm_ref[rows // 2 :]

    return call(
        kernel,
        [shape((3, rows, columns), BF)] + [shape((rows // 2, columns), BF)] * 2,
        x2,
        zm,
        zp,
    )


def cut_halves(up, down, weight=0):
    count = up.shape[0] // 2
    cut = shape((count,) + up.shape[1:], up.dtype)

    def kernel(up_ref, down_ref, a_ref, b_ref):
        a_ref[...] = up_ref[:count]
        b_ref[...] = down_ref[count:]

    return call(kernel, [cut, cut], up, down, weight=weight)


def reduce_kernel(pieces_ref, out_ref):
    total = pieces_ref[0].astype(F32)
    for i in range(1, pieces_ref.shape[0]):
        total += pieces_ref[i].astype(F32)
    out_ref[...] = total.T.astype(BF)


def reduce_pieces(pieces):
    count, half, width = pieces.shape
    return call(reduce_kernel, shape((width, half), BF), pieces)


def chip_at(i, j, core):
    z, x, _ = place()
    dx = jnp.where(core == 0, REL[i], REL[j])
    dz = jnp.where(core == 0, REL[j], REL[i])
    return (z + dz + 4) % 4, (x + dx + 4) % 4


def root_sum(entries, p_ref, r_refs, total):
    rows = p_ref.shape[0]
    core = place()[2]
    for k, r_ref in enumerate(r_refs):
        owner = core if k < len(entries) else 1 - core
        for n, (i, j) in enumerate(entries[k % len(entries)]):
            z, x = chip_at(i, j, owner)
            at = pl.multiple_of((z * 8 + x * 2 + owner) * rows, BLK)
            part = jnp.dot(p_ref[:, pl.ds(at, rows)], r_ref[n], preferred_element_type=F32)
            total = part if total is None else total + part
    return total


def base_product(blocks, inverse, near, far):
    rows, columns = inverse.shape[0], near[0].shape[2]

    def kernel(blocks_ref, p_ref, *refs):
        r_refs, (out_ref, picked_ref) = refs[:-2], refs[-2:]
        total = root_sum(NEAR, p_ref, r_refs[: len(near)], None)
        out_ref[...] = root_sum(FAR, p_ref, r_refs[len(near) :], total)
        core = place()[2]
        for n in range(picked_ref.shape[1] // BLK):
            z, x = chip_at(n // 3 % 4, n // 12, core)
            block = blocks_ref[z // 2, (z % 2 * 4 + x) * 3 + n % 3]
            at = pl.multiple_of(block * BLK, BLK)
            picked_ref[:, n * BLK : (n + 1) * BLK] = p_ref[:, pl.ds(at, BLK)]

    return call(
        kernel,
        [shape((rows, columns), F32), shape((rows, blocks.size * BLK), inverse.dtype)],
        blocks,
        inverse,
        *near,
        *far,
        smem=1,
    )


def final_kernel(base_ref, p_ref, *refs):
    own_refs, sib_refs, out_ref = refs[:4], refs[4:8], refs[8]
    width, half = own_refs[0].shape[1:]
    total = base_ref[...]
    change = None
    for j in range(4):
        for i in range(4):
            block = jnp.concatenate([own_refs[j][i], sib_refs[i][j]], axis=1)
            at = (j * 4 + i) * width
            part = jnp.dot(p_ref[:, at : at + width], block, preferred_element_type=F32)
            change = part if change is None else change + part
    core = place()[2]

    @pl.when(core == 0)
    def _():
        out_ref[...] = (total - change).T

    @pl.when(core == 1)
    def _():
        out_ref[:half] = (total[:, :half] - change[:, half:]).T
        out_ref[half:] = (total[:, half:] - change[:, :half]).T


def final_product(base, picked, own, sib):
    rows, columns = base.shape
    return call(
        final_kernel,
        shape((columns, rows), F32),
        base,
        picked,
        *own,
        *sib,
    )


def gather_first(block):
    return [block] + [receive(block, along(s, True)) for s in STEPS]


def gather_second(first):
    part = jnp.stack(first)
    return [part] + [receive(part, along(s, False)) for s in STEPS]


def gather_near(first):
    part = jnp.stack(first)
    return [part] + [receive(part, along(s, False)) for s in STEPS[:2]]


def gather_far(up, down):
    return [receive(up, along(1, False)), receive(down, along(-1, False))]


NEAR = [[(i, j) for i in range(4)] for j in range(3)]
FAR = [[(0, 3), (1, 3)], [(2, 3), (3, 3)]]


def on_device(
    child_rhs, parent_rhs, child_inverse, coupling, parent_inverse, child_blocks, parent_block
):
    b0 = child_rhs.T.astype(BF)
    b0_sib = from_sibling(b0)
    xp = receive(b0, lambda z, x, c: (z, x + 1, c))
    xm = receive(b0, lambda z, x, c: (z, x - 1, c))
    zb = receive(b0, lambda z, x, c: (z ^ 1, x, c))
    (child_inverse,) = load(child_inverse)
    xp, xm, zb, b0_sib, child_inverse, coupling, parent_rhs = tie(
        xp, xm, zb, b0_sib, child_inverse, coupling, parent_rhs
    )
    near = pile(xp, xm, zb)
    near_sib = from_sibling(near)
    parent_rhs, coupling, near_sib = tie(parent_rhs, coupling, near_sib)
    root = turn(parent_rhs)
    (coupling,) = load(coupling)
    acc = child_part([(0, 0), (0, 1), (0, 3), (1, 0)], child_inverse, [b0, near, b0_sib, near_sib])
    x2 = receive(xp, lambda z, x, c: (z, x + 1, c))
    zm = receive(zb, lambda z, x, c: (z, x - 1, c))
    zp = receive(xp, lambda z, x, c: (z ^ 1, x, c))
    r_first = [root] + [receive(root, along(s, True)) for s in STEPS[:2]]
    x2, zm, zp, acc, coupling, *r_first = tie(x2, zm, zp, acc, coupling, *r_first)
    mid, last_a, last_b = pile_and_cut(x2, zm, zp)
    acc = child_part([(0, 2), (1, 3), (1, 1)], child_inverse, [mid, from_sibling(mid)], acc)
    r_near = gather_near(r_first + [receive(r_first[1], along(1, True))])
    z2 = jnp.concatenate(
        [
            receive(last_a, lambda z, x, c: (z, x + 1, c)),
            receive(last_b, lambda z, x, c: (z, x - 1, c)),
        ],
        axis=0,
    )
    z2, acc = tie(z2, acc)
    solution_t, keep, *give = child_last(
        [(1, 2)], [z2, from_sibling(z2)], acc, child_inverse, coupling, child_blocks, 8
    )

    got = jnp.concatenate([from_sibling(part) for part in give], axis=0)
    chip_sum = (keep + got.astype(F32)).astype(BF)
    groups = [
        [flat(2 * h + dz, xx, c) for dz in range(2) for xx in range(4)]
        for h in range(2)
        for c in range(2)
    ]
    far_up, far_down = cut_halves(r_near[1], r_near[2], weight=2 << 20)
    chip_sum, far_up, far_down, *r_near = tie(chip_sum, far_up, far_down, *r_near)
    pieces = lax.all_to_all(
        chip_sum, "wide", split_axis=0, concat_axis=0, axis_index_groups=groups, tiled=True
    )
    r_far = gather_far(far_up, far_down)
    update, *r_sib = tie(reduce_pieces(pieces), *[from_sibling(part) for part in r_near])
    r_near += r_sib
    update, parent_inverse = tie(update, parent_inverse)
    (parent_inverse,) = load(parent_inverse)
    *u_first, parent_inverse, r_far[0], r_far[1] = tie(
        *gather_first(update), parent_inverse, *r_far
    )
    r_far += [from_sibling(part) for part in r_far]
    u_own = gather_second(u_first)
    u_sib = [from_sibling(u_own[0])]
    base, picked = base_product(parent_block, parent_inverse, r_near, r_far)
    base, u_own[1], u_sib[0] = tie(base, u_own[1], u_sib[0])
    u_sib += [from_sibling(part) for part in u_own[1:]]
    parent_solution = final_product(base, picked, u_own, u_sib)
    return (solution_t.T, parent_solution)


def solution(mesh):
    placed = (
        P("rhs", "wide"),
        P("rhs", "wide"),
        P("wide", None),
        P("wide", None),
        P("wide", None),
        P(),
        P(),
    )
    return jax.shard_map(
        on_device,
        mesh=mesh,
        in_specs=placed,
        out_specs=(P("rhs", "wide"), P("rhs", "wide")),
        check_vma=False,
    )
```

```python
import functools

import jax
import jax.numpy as jnp
from jax import lax
from jax.experimental import pallas as pl
from jax.experimental.pallas import tpu as pltpu
from jax.sharding import PartitionSpec as P

BLK = 128
BF = jnp.bfloat16
F32 = jnp.float32
BANDS = 8
VMEM_LIMIT = 8 * 1024 * 1024


def flat(z, x, c):
    return (z % 4) * 8 + (x % 4) * 2 + c


def receive(value, source):
    pairs = []
    for z in range(4):
        for x in range(4):
            for c in range(2):
                pairs.append((flat(*source(z, x, c)), flat(z, x, c)))
    return lax.ppermute(value, "wide", pairs)


def from_sibling(value):
    return receive(value, lambda z, x, c: (z, x, 1 - c))


def tie(*values):
    return lax.optimization_barrier(values)


STEPS = (1, -1, 2)
REL = (0, 1, -1, 2)


def along(step, first):
    def source(z, x, c):
        return (z, x + step, c) if (c == 0) == first else (z + step, x, c)

    return source


VMEM = pl.BlockSpec(memory_space=pltpu.VMEM)
SMEM = pl.BlockSpec(memory_space=pltpu.SMEM)


HBM = pl.BlockSpec(memory_space=pltpu.HBM)


def call(kernel, out_shape, *operands, smem=0, hbm=(), scratch=(), weight=0):
    specs = [SMEM if i < smem else HBM if i in hbm else VMEM for i in range(len(operands))]
    operands = [
        pltpu.with_memory_space_constraint(operand, pltpu.HBM) if i in hbm else operand
        for i, operand in enumerate(operands)
    ]
    return pl.pallas_call(
        kernel,
        in_specs=specs,
        out_specs=jax.tree.map(lambda _: VMEM, out_shape),
        out_shape=out_shape,
        scratch_shapes=scratch,
        compiler_params=pltpu.CompilerParams(vmem_limit_bytes=VMEM_LIMIT),
        cost_estimate=pl.CostEstimate(flops=0, bytes_accessed=weight, transcendentals=0),
    )(*operands)


def shape(dims, dtype):
    return jax.ShapeDtypeStruct(dims, dtype)


def load_kernel(count, sources, *refs):
    targets, sems = refs[:count], refs[count]
    copies = []
    for k in range(count):
        band = sources[k].shape[0] // BANDS
        for i in range(BANDS):
            rows = pl.ds(i * band, band)
            copies.append(
                pltpu.make_async_copy(sources[k].at[rows], targets[k].at[rows], sems.at[k, i])
            )
    for copy in copies:
        copy.start()
    for copy in copies:
        copy.wait()


def load(*arrays):
    count = len(arrays)

    def kernel(*refs):
        load_kernel(count, refs[:count], *refs[count:])

    return call(
        kernel,
        [shape(a.shape, a.dtype) for a in arrays],
        *arrays,
        hbm=range(count),
        scratch=[pltpu.SemaphoreType.DMA((count, BANDS))],
    )


def place():
    rank = lax.axis_index("wide")
    return rank // 8, rank // 2 % 4, rank % 2


def part_sum(chips, inv_ref, block_refs, held_ref, total):
    rows = inv_ref.shape[0]
    z, x, core = place()
    mine = pl.ds(pl.multiple_of(core * rows, 16), rows)
    others = pl.ds(pl.multiple_of((1 - core) * rows, 16), rows)
    for i, (dz, dx) in enumerate(chips):
        held_ref[i, mine] = block_refs[i]
        held_ref[i, others] = block_refs[len(chips) + i]
        at = ((z + dz) % 2 * 4 + (x + dx) % 4) * 2 * rows
        columns = pl.ds(pl.multiple_of(at, BLK), 2 * rows)
        part = jnp.dot(inv_ref[:, columns], held_ref[i], preferred_element_type=F32)
        total = part if total is None else total + part
    return total


def held_scratch(chips, inverse, columns):
    return pltpu.VMEM((len(chips), 2 * inverse.shape[0], columns), BF)


def entries(refs):
    blocks = []
    for ref in refs:
        blocks += [ref[...]] if len(ref.shape) == 2 else [ref[i] for i in range(ref.shape[0])]
    return blocks


def child_part(chips, inverse, blocks, *acc):
    rows, columns = blocks[0].shape[-2:]
    count = len(blocks)

    def kernel(inv_ref, *refs):
        block_refs, refs = refs[:count], refs[count:]
        start = refs[0][...] if acc else None
        out_ref, held_ref = refs[-2:]
        out_ref[...] = part_sum(chips, inv_ref, entries(block_refs), held_ref, start)

    return call(
        kernel,
        shape((rows, columns), F32),
        inverse,
        *blocks,
        *acc,
        scratch=[held_scratch(chips, inverse, columns)],
    )


def child_last(chips, blocks, acc, inverse, coupling, child_blocks, pieces):
    rows, columns = acc.shape
    half, width = columns // 2, coupling.shape[1] // pieces
    count = len(blocks)

    def kernel(sizes_ref, inv_ref, coupling_ref, acc_ref, *refs):
        block_refs, refs = refs[:count], refs[count:]
        out_ref, keep_ref, *give_refs, held_ref, solved_ref = refs
        total = part_sum(chips, inv_ref, entries(block_refs), held_ref, acc_ref[...])
        z, x, core = place()
        row = lax.broadcasted_iota(jnp.int32, total.shape, 0)
        first = (z % 2 * 8 + x * 2 + core) * rows
        limit = BLK * sizes_ref[z // 2] - first
        total = jnp.where(row < limit, total, 0.0)
        out_ref[...] = total
        solved_ref[...] = total.T.astype(BF)
        mine = pl.ds(pl.multiple_of(core * half, half), half)
        others = pl.ds(pl.multiple_of((1 - core) * half, half), half)
        solved = jnp.concatenate([solved_ref[mine], solved_ref[others]], axis=0)
        for i in range(pieces):
            update = jnp.dot(
                solved, coupling_ref[:, i * width : (i + 1) * width], preferred_element_type=F32
            )
            keep_ref[i] = update[:half]
            give_refs[2 * i // pieces][i % (pieces // 2)] = update[half:].astype(BF)

    return call(
        kernel,
        [
            shape((rows, columns), F32),
            shape((pieces, half, width), F32),
        ]
        + [shape((pieces // 2, half, width), BF)] * 2,
        child_blocks,
        inverse,
        coupling,
        acc,
        *blocks,
        smem=1,
        scratch=[held_scratch(chips, inverse, columns), pltpu.VMEM((columns, rows), BF)],
    )


def turn(block):
    def kernel(block_ref, out_ref):
        out_ref[...] = block_ref[...].T.astype(BF)

    return call(kernel, shape(block.shape[::-1], BF), block)


def pile(*blocks):
    def kernel(*refs):
        for i, ref in enumerate(refs[:-1]):
            refs[-1][i] = ref[...]

    return call(kernel, shape((len(blocks),) + blocks[0].shape, BF), *blocks)


def pile_and_cut(x2, zm, zp):
    rows, columns = x2.shape

    def kernel(x2_ref, zm_ref, zp_ref, pile_ref, a_ref, b_ref):
        for i, ref in enumerate((x2_ref, zm_ref, zp_ref)):
            pile_ref[i] = ref[...]
        a_ref[...] = zp_ref[: rows // 2]
        b_ref[...] = zm_ref[rows // 2 :]

    return call(
        kernel,
        [shape((3, rows, columns), BF)] + [shape((rows // 2, columns), BF)] * 2,
        x2,
        zm,
        zp,
    )


def cut_halves(up, down, weight=0):
    count = up.shape[0] // 2
    cut = shape((count,) + up.shape[1:], up.dtype)

    def kernel(up_ref, down_ref, a_ref, b_ref):
        a_ref[...] = up_ref[:count]
        b_ref[...] = down_ref[count:]

    return call(kernel, [cut, cut], up, down, weight=weight)


def reduce_kernel(pieces_ref, out_ref):
    total = pieces_ref[0].astype(F32)
    for i in range(1, pieces_ref.shape[0]):
        total += pieces_ref[i].astype(F32)
    out_ref[...] = total.T.astype(BF)


def reduce_pieces(pieces):
    count, half, width = pieces.shape
    return call(reduce_kernel, shape((width, half), BF), pieces)


def chip_at(i, j, core):
    z, x, _ = place()
    dx = jnp.where(core == 0, REL[i], REL[j])
    dz = jnp.where(core == 0, REL[j], REL[i])
    return (z + dz + 4) % 4, (x + dx + 4) % 4


def root_sum(entries, p_ref, r_refs, total):
    rows = p_ref.shape[0]
    core = place()[2]
    for k, r_ref in enumerate(r_refs):
        owner = core if k < len(entries) else 1 - core
        for n, (i, j) in enumerate(entries[k % len(entries)]):
            z, x = chip_at(i, j, owner)
            at = pl.multiple_of((z * 8 + x * 2 + owner) * rows, BLK)
            part = jnp.dot(p_ref[:, pl.ds(at, rows)], r_ref[n], preferred_element_type=F32)
            total = part if total is None else total + part
    return total


def base_product(blocks, inverse, near, far):
    rows, columns = inverse.shape[0], near[0].shape[2]

    def kernel(blocks_ref, p_ref, *refs):
        r_refs, (out_ref, picked_ref) = refs[:-2], refs[-2:]
        total = root_sum(NEAR, p_ref, r_refs[: len(near)], None)
        out_ref[...] = root_sum(FAR, p_ref, r_refs[len(near) :], total)
        core = place()[2]
        for n in range(picked_ref.shape[1] // BLK):
            z, x = chip_at(n // 3 % 4, n // 12, core)
            block = blocks_ref[z // 2, (z % 2 * 4 + x) * 3 + n % 3]
            at = pl.multiple_of(block * BLK, BLK)
            picked_ref[:, n * BLK : (n + 1) * BLK] = p_ref[:, pl.ds(at, BLK)]

    return call(
        kernel,
        [shape((rows, columns), F32), shape((rows, blocks.size * BLK), inverse.dtype)],
        blocks,
        inverse,
        *near,
        *far,
        smem=1,
        weight=7 << 19,
    )


def final_kernel(base_ref, p_ref, *refs):
    own_refs, sib_refs, out_ref, held_ref = refs[:4], refs[4:8], refs[8], refs[9]
    width, half = own_refs[0].shape[1:]
    total = base_ref[...]
    for j in range(4):
        for i in range(4):
            rows = pl.ds((j * 4 + i) * width, width)
            held_ref[rows, :half] = own_refs[j][i]
            held_ref[rows, half:] = sib_refs[i][j]
    change = jnp.dot(p_ref[...], held_ref[...], preferred_element_type=F32)
    core = place()[2]

    @pl.when(core == 0)
    def _():
        out_ref[...] = (total - change).T

    @pl.when(core == 1)
    def _():
        out_ref[:half] = (total[:, :half] - change[:, half:]).T
        out_ref[half:] = (total[:, half:] - change[:, :half]).T


def final_product(base, picked, own, sib):
    rows, columns = base.shape
    return call(
        final_kernel,
        shape((columns, rows), F32),
        base,
        picked,
        *own,
        *sib,
        scratch=[pltpu.VMEM((picked.shape[1], columns), BF)],
    )


def gather_first(block):
    return [block] + [receive(block, along(s, True)) for s in STEPS]


def gather_second(first):
    part = jnp.stack(first)
    return [part] + [receive(part, along(s, False)) for s in STEPS]


def gather_near(first):
    part = jnp.stack(first)
    return [part] + [receive(part, along(s, False)) for s in STEPS[:2]]


def gather_far(up, down):
    return [receive(up, along(1, False)), receive(down, along(-1, False))]


NEAR = [[(i, j) for i in range(4)] for j in range(3)]
FAR = [[(0, 3), (1, 3)], [(2, 3), (3, 3)]]


def on_device(
    child_rhs, parent_rhs, child_inverse, coupling, parent_inverse, child_blocks, parent_block
):
    b0 = child_rhs.T.astype(BF)
    b0_sib = from_sibling(b0)
    xp = receive(b0, lambda z, x, c: (z, x + 1, c))
    xm = receive(b0, lambda z, x, c: (z, x - 1, c))
    zb = receive(b0, lambda z, x, c: (z ^ 1, x, c))
    (child_inverse,) = load(child_inverse)
    xp, xm, zb, b0_sib, child_inverse, coupling, parent_rhs = tie(
        xp, xm, zb, b0_sib, child_inverse, coupling, parent_rhs
    )
    near = pile(xp, xm, zb)
    near_sib = from_sibling(near)
    parent_rhs, coupling, near_sib = tie(parent_rhs, coupling, near_sib)
    root = turn(parent_rhs)
    (coupling,) = load(coupling)
    acc = child_part([(0, 0), (0, 1), (0, 3), (1, 0)], child_inverse, [b0, near, b0_sib, near_sib])
    x2 = receive(xp, lambda z, x, c: (z, x + 1, c))
    zm = receive(zb, lambda z, x, c: (z, x - 1, c))
    zp = receive(xp, lambda z, x, c: (z ^ 1, x, c))
    r_first = [root] + [receive(root, along(s, True)) for s in STEPS[:2]]
    x2, zm, zp, acc, coupling, *r_first = tie(x2, zm, zp, acc, coupling, *r_first)
    mid, last_a, last_b = pile_and_cut(x2, zm, zp)
    acc = child_part([(0, 2), (1, 3), (1, 1)], child_inverse, [mid, from_sibling(mid)], acc)
    r_near = gather_near(r_first + [receive(r_first[1], along(1, True))])
    z2 = jnp.concatenate(
        [
            receive(last_a, lambda z, x, c: (z, x + 1, c)),
            receive(last_b, lambda z, x, c: (z, x - 1, c)),
        ],
        axis=0,
    )
    z2, acc = tie(z2, acc)
    solution_t, keep, *give = child_last(
        [(1, 2)], [z2, from_sibling(z2)], acc, child_inverse, coupling, child_blocks, 8
    )

    got = jnp.concatenate([from_sibling(part) for part in give], axis=0)
    chip_sum = (keep + got.astype(F32)).astype(BF)
    groups = [
        [flat(2 * h + dz, xx, c) for dz in range(2) for xx in range(4)]
        for h in range(2)
        for c in range(2)
    ]
    far_up, far_down = cut_halves(r_near[1], r_near[2], weight=2 << 20)
    chip_sum, far_up, far_down, *r_near = tie(chip_sum, far_up, far_down, *r_near)
    pieces = lax.all_to_all(
        chip_sum, "wide", split_axis=0, concat_axis=0, axis_index_groups=groups, tiled=True
    )
    r_far = gather_far(far_up, far_down)
    update, *r_sib = tie(reduce_pieces(pieces), *[from_sibling(part) for part in r_near])
    r_near += r_sib
    update, parent_inverse = tie(update, parent_inverse)
    (parent_inverse,) = load(parent_inverse)
    *u_first, parent_inverse, r_far[0], r_far[1] = tie(
        *gather_first(update), parent_inverse, *r_far
    )
    r_far += [from_sibling(part) for part in r_far]
    u_own = gather_second(u_first)
    u_sib = [from_sibling(u_own[0])]
    base, picked = base_product(parent_block, parent_inverse, r_near, r_far)
    base, u_own[1], u_sib[0] = tie(base, u_own[1], u_sib[0])
    u_sib += [from_sibling(part) for part in u_own[1:]]
    parent_solution = final_product(base, picked, u_own, u_sib)
    return (solution_t.T, parent_solution)


def solution(mesh):
    placed = (
        P("rhs", "wide"),
        P("rhs", "wide"),
        P("wide", None),
        P("wide", None),
        P("wide", None),
        P(),
        P(),
    )
    return jax.shard_map(
        on_device,
        mesh=mesh,
        in_specs=placed,
        out_specs=(P("rhs", "wide"), P("rhs", "wide")),
        check_vma=False,
    )
```

```python
import functools

import jax
import jax.numpy as jnp
from jax import lax
from jax.experimental import pallas as pl
from jax.experimental.pallas import tpu as pltpu
from jax.sharding import PartitionSpec as P

BLK = 128
BF = jnp.bfloat16
F32 = jnp.float32
BANDS = 8
VMEM_LIMIT = 8 * 1024 * 1024


def flat(z, x, c):
    return (z % 4) * 8 + (x % 4) * 2 + c


def receive(value, source):
    pairs = []
    for z in range(4):
        for x in range(4):
            for c in range(2):
                pairs.append((flat(*source(z, x, c)), flat(z, x, c)))
    return lax.ppermute(value, "wide", pairs)


def from_sibling(value):
    return receive(value, lambda z, x, c: (z, x, 1 - c))


def tie(*values):
    return lax.optimization_barrier(values)


STEPS = (1, -1, 2)
REL = (0, 1, -1, 2)


def along(step, first):
    def source(z, x, c):
        return (z, x + step, c) if (c == 0) == first else (z + step, x, c)

    return source


VMEM = pl.BlockSpec(memory_space=pltpu.VMEM)
SMEM = pl.BlockSpec(memory_space=pltpu.SMEM)


HBM = pl.BlockSpec(memory_space=pltpu.HBM)


def call(kernel, out_shape, *operands, smem=0, hbm=(), scratch=(), weight=0):
    specs = [SMEM if i < smem else HBM if i in hbm else VMEM for i in range(len(operands))]
    operands = [
        pltpu.with_memory_space_constraint(operand, pltpu.HBM) if i in hbm else operand
        for i, operand in enumerate(operands)
    ]
    return pl.pallas_call(
        kernel,
        in_specs=specs,
        out_specs=jax.tree.map(lambda _: VMEM, out_shape),
        out_shape=out_shape,
        scratch_shapes=scratch,
        compiler_params=pltpu.CompilerParams(vmem_limit_bytes=VMEM_LIMIT),
        cost_estimate=pl.CostEstimate(flops=0, bytes_accessed=weight, transcendentals=0),
    )(*operands)


def shape(dims, dtype):
    return jax.ShapeDtypeStruct(dims, dtype)


def load_kernel(count, sources, *refs):
    targets, sems = refs[:count], refs[count]
    copies = []
    for k in range(count):
        band = sources[k].shape[0] // BANDS
        for i in range(BANDS):
            rows = pl.ds(i * band, band)
            copies.append(
                pltpu.make_async_copy(sources[k].at[rows], targets[k].at[rows], sems.at[k, i])
            )
    for copy in copies:
        copy.start()
    for copy in copies:
        copy.wait()


def load(*arrays):
    count = len(arrays)

    def kernel(*refs):
        load_kernel(count, refs[:count], *refs[count:])

    return call(
        kernel,
        [shape(a.shape, a.dtype) for a in arrays],
        *arrays,
        hbm=range(count),
        scratch=[pltpu.SemaphoreType.DMA((count, BANDS))],
    )


def place():
    rank = lax.axis_index("wide")
    return rank // 8, rank // 2 % 4, rank % 2


def part_sum(chips, inv_ref, block_refs, held_ref, total):
    rows = inv_ref.shape[0]
    z, x, core = place()
    mine = pl.ds(pl.multiple_of(core * rows, 16), rows)
    others = pl.ds(pl.multiple_of((1 - core) * rows, 16), rows)
    for i, (dz, dx) in enumerate(chips):
        held_ref[i, mine] = block_refs[i]
        held_ref[i, others] = block_refs[len(chips) + i]
        at = ((z + dz) % 2 * 4 + (x + dx) % 4) * 2 * rows
        columns = pl.ds(pl.multiple_of(at, BLK), 2 * rows)
        part = jnp.dot(inv_ref[:, columns], held_ref[i], preferred_element_type=F32)
        total = part if total is None else total + part
    return total


def held_scratch(chips, inverse, columns):
    return pltpu.VMEM((len(chips), 2 * inverse.shape[0], columns), BF)


def entries(refs):
    blocks = []
    for ref in refs:
        blocks += [ref[...]] if len(ref.shape) == 2 else [ref[i] for i in range(ref.shape[0])]
    return blocks


def child_part(chips, inverse, blocks, *acc):
    rows, columns = blocks[0].shape[-2:]
    count = len(blocks)

    def kernel(inv_ref, *refs):
        block_refs, refs = refs[:count], refs[count:]
        start = refs[0][...] if acc else None
        out_ref, held_ref = refs[-2:]
        out_ref[...] = part_sum(chips, inv_ref, entries(block_refs), held_ref, start)

    return call(
        kernel,
        shape((rows, columns), F32),
        inverse,
        *blocks,
        *acc,
        scratch=[held_scratch(chips, inverse, columns)],
    )


def child_last(chips, blocks, acc, inverse, coupling, child_blocks, pieces):
    rows, columns = acc.shape
    half, width = columns // 2, coupling.shape[1] // pieces
    count = len(blocks)

    def kernel(sizes_ref, inv_ref, coupling_ref, acc_ref, *refs):
        block_refs, refs = refs[:count], refs[count:]
        out_ref, keep_ref, *give_refs, held_ref, solved_ref = refs
        total = part_sum(chips, inv_ref, entries(block_refs), held_ref, acc_ref[...])
        z, x, core = place()
        row = lax.broadcasted_iota(jnp.int32, total.shape, 0)
        first = (z % 2 * 8 + x * 2 + core) * rows
        limit = BLK * sizes_ref[z // 2] - first
        total = jnp.where(row < limit, total, 0.0)
        out_ref[...] = total
        solved_ref[...] = total.T.astype(BF)
        mine = pl.ds(pl.multiple_of(core * half, half), half)
        others = pl.ds(pl.multiple_of((1 - core) * half, half), half)
        solved = jnp.concatenate([solved_ref[mine], solved_ref[others]], axis=0)
        per_half = pieces // 2
        for k in range(2):
            columns_k = slice(k * per_half * width, (k + 1) * per_half * width)
            update = jnp.dot(solved, coupling_ref[:, columns_k], preferred_element_type=F32)
            for i in range(per_half):
                piece = update[:, i * width : (i + 1) * width]
                keep_ref[k * per_half + i] = piece[:half]
                give_refs[k][i] = piece[half:].astype(BF)

    return call(
        kernel,
        [
            shape((rows, columns), F32),
            shape((pieces, half, width), F32),
        ]
        + [shape((pieces // 2, half, width), BF)] * 2,
        child_blocks,
        inverse,
        coupling,
        acc,
        *blocks,
        smem=1,
        scratch=[held_scratch(chips, inverse, columns), pltpu.VMEM((columns, rows), BF)],
    )


def turn(block):
    def kernel(block_ref, out_ref):
        out_ref[...] = block_ref[...].T.astype(BF)

    return call(kernel, shape(block.shape[::-1], BF), block)


def pile(*blocks):
    def kernel(*refs):
        for i, ref in enumerate(refs[:-1]):
            refs[-1][i] = ref[...]

    return call(kernel, shape((len(blocks),) + blocks[0].shape, BF), *blocks)


def pile_and_cut(x2, zm, zp):
    rows, columns = x2.shape

    def kernel(x2_ref, zm_ref, zp_ref, pile_ref, a_ref, b_ref):
        for i, ref in enumerate((x2_ref, zm_ref, zp_ref)):
            pile_ref[i] = ref[...]
        a_ref[...] = zp_ref[: rows // 2]
        b_ref[...] = zm_ref[rows // 2 :]

    return call(
        kernel,
        [shape((3, rows, columns), BF)] + [shape((rows // 2, columns), BF)] * 2,
        x2,
        zm,
        zp,
    )


def cut_halves(up, down, weight=0):
    count = up.shape[0] // 2
    cut = shape((count,) + up.shape[1:], up.dtype)

    def kernel(up_ref, down_ref, a_ref, b_ref):
        a_ref[...] = up_ref[:count]
        b_ref[...] = down_ref[count:]

    return call(kernel, [cut, cut], up, down, weight=weight)


def reduce_kernel(pieces_ref, out_ref):
    total = pieces_ref[0].astype(F32)
    for i in range(1, pieces_ref.shape[0]):
        total += pieces_ref[i].astype(F32)
    out_ref[...] = total.T.astype(BF)


def reduce_pieces(pieces):
    count, half, width = pieces.shape
    return call(reduce_kernel, shape((width, half), BF), pieces)


def chip_at(i, j, core):
    z, x, _ = place()
    dx = jnp.where(core == 0, REL[i], REL[j])
    dz = jnp.where(core == 0, REL[j], REL[i])
    return (z + dz + 4) % 4, (x + dx + 4) % 4


def root_sum(entries, p_ref, r_refs, total):
    rows = p_ref.shape[0]
    core = place()[2]
    for k, r_ref in enumerate(r_refs):
        owner = core if k < len(entries) else 1 - core
        for n, (i, j) in enumerate(entries[k % len(entries)]):
            z, x = chip_at(i, j, owner)
            at = pl.multiple_of((z * 8 + x * 2 + owner) * rows, BLK)
            part = jnp.dot(p_ref[:, pl.ds(at, rows)], r_ref[n], preferred_element_type=F32)
            total = part if total is None else total + part
    return total


def base_product(blocks, inverse, near, far):
    rows, columns = inverse.shape[0], near[0].shape[2]

    def kernel(blocks_ref, p_ref, *refs):
        r_refs, (out_ref, picked_ref) = refs[:-2], refs[-2:]
        total = root_sum(NEAR, p_ref, r_refs[: len(near)], None)
        out_ref[...] = root_sum(FAR, p_ref, r_refs[len(near) :], total)
        core = place()[2]
        for n in range(picked_ref.shape[1] // BLK):
            z, x = chip_at(n // 3 % 4, n // 12, core)
            block = blocks_ref[z // 2, (z % 2 * 4 + x) * 3 + n % 3]
            at = pl.multiple_of(block * BLK, BLK)
            picked_ref[:, n * BLK : (n + 1) * BLK] = p_ref[:, pl.ds(at, BLK)]

    return call(
        kernel,
        [shape((rows, columns), F32), shape((rows, blocks.size * BLK), inverse.dtype)],
        blocks,
        inverse,
        *near,
        *far,
        smem=1,
        weight=7 << 19,
    )


def final_kernel(base_ref, p_ref, *refs):
    own_refs, sib_refs, out_ref, held_ref = refs[:4], refs[4:8], refs[8], refs[9]
    width, half = own_refs[0].shape[1:]
    total = base_ref[...]
    for j in range(4):
        for i in range(4):
            rows = pl.ds((j * 4 + i) * width, width)
            held_ref[rows, :half] = own_refs[j][i]
            held_ref[rows, half:] = sib_refs[i][j]
    change = jnp.dot(p_ref[...], held_ref[...], preferred_element_type=F32)
    core = place()[2]

    @pl.when(core == 0)
    def _():
        out_ref[...] = (total - change).T

    @pl.when(core == 1)
    def _():
        out_ref[:half] = (total[:, :half] - change[:, half:]).T
        out_ref[half:] = (total[:, half:] - change[:, :half]).T


def final_product(base, picked, own, sib):
    rows, columns = base.shape
    return call(
        final_kernel,
        shape((columns, rows), F32),
        base,
        picked,
        *own,
        *sib,
        scratch=[pltpu.VMEM((picked.shape[1], columns), BF)],
    )


def gather_first(block):
    return [block] + [receive(block, along(s, True)) for s in STEPS]


def gather_second(first):
    part = jnp.stack(first)
    return [part] + [receive(part, along(s, False)) for s in STEPS]


def gather_near(first):
    part = jnp.stack(first)
    return [part] + [receive(part, along(s, False)) for s in STEPS[:2]]


def gather_far(up, down):
    return [receive(up, along(1, False)), receive(down, along(-1, False))]


NEAR = [[(i, j) for i in range(4)] for j in range(3)]
FAR = [[(0, 3), (1, 3)], [(2, 3), (3, 3)]]


def on_device(
    child_rhs, parent_rhs, child_inverse, coupling, parent_inverse, child_blocks, parent_block
):
    b0 = child_rhs.T.astype(BF)
    b0_sib = from_sibling(b0)
    xp = receive(b0, lambda z, x, c: (z, x + 1, c))
    xm = receive(b0, lambda z, x, c: (z, x - 1, c))
    zb = receive(b0, lambda z, x, c: (z ^ 1, x, c))
    (child_inverse,) = load(child_inverse)
    xp, xm, zb, b0_sib, child_inverse, coupling, parent_rhs = tie(
        xp, xm, zb, b0_sib, child_inverse, coupling, parent_rhs
    )
    near = pile(xp, xm, zb)
    near_sib = from_sibling(near)
    parent_rhs, coupling, near_sib = tie(parent_rhs, coupling, near_sib)
    root = turn(parent_rhs)
    (coupling,) = load(coupling)
    acc = child_part([(0, 0), (0, 1), (0, 3), (1, 0)], child_inverse, [b0, near, b0_sib, near_sib])
    x2 = receive(xp, lambda z, x, c: (z, x + 1, c))
    zm = receive(zb, lambda z, x, c: (z, x - 1, c))
    zp = receive(xp, lambda z, x, c: (z ^ 1, x, c))
    r_first = [root] + [receive(root, along(s, True)) for s in STEPS[:2]]
    x2, zm, zp, acc, coupling, *r_first = tie(x2, zm, zp, acc, coupling, *r_first)
    mid, last_a, last_b = pile_and_cut(x2, zm, zp)
    acc = child_part([(0, 2), (1, 3), (1, 1)], child_inverse, [mid, from_sibling(mid)], acc)
    r_near = gather_near(r_first + [receive(r_first[1], along(1, True))])
    z2 = jnp.concatenate(
        [
            receive(last_a, lambda z, x, c: (z, x + 1, c)),
            receive(last_b, lambda z, x, c: (z, x - 1, c)),
        ],
        axis=0,
    )
    z2, acc = tie(z2, acc)
    solution_t, keep, *give = child_last(
        [(1, 2)], [z2, from_sibling(z2)], acc, child_inverse, coupling, child_blocks, 8
    )

    got = jnp.concatenate([from_sibling(part) for part in give], axis=0)
    chip_sum = (keep + got.astype(F32)).astype(BF)
    groups = [
        [flat(2 * h + dz, xx, c) for dz in range(2) for xx in range(4)]
        for h in range(2)
        for c in range(2)
    ]
    far_up, far_down = cut_halves(r_near[1], r_near[2], weight=2 << 20)
    chip_sum, far_up, far_down, *r_near = tie(chip_sum, far_up, far_down, *r_near)
    pieces = lax.all_to_all(
        chip_sum, "wide", split_axis=0, concat_axis=0, axis_index_groups=groups, tiled=True
    )
    r_far = gather_far(far_up, far_down)
    update, *r_sib = tie(reduce_pieces(pieces), *[from_sibling(part) for part in r_near])
    r_near += r_sib
    update, parent_inverse = tie(update, parent_inverse)
    (parent_inverse,) = load(parent_inverse)
    *u_first, parent_inverse, r_far[0], r_far[1] = tie(
        *gather_first(update), parent_inverse, *r_far
    )
    r_far += [from_sibling(part) for part in r_far]
    u_own = gather_second(u_first)
    u_sib = [from_sibling(u_own[0])]
    base, picked = base_product(parent_block, parent_inverse, r_near, r_far)
    base, u_own[1], u_sib[0] = tie(base, u_own[1], u_sib[0])
    u_sib += [from_sibling(part) for part in u_own[1:]]
    parent_solution = final_product(base, picked, u_own, u_sib)
    return (solution_t.T, parent_solution)


def solution(mesh):
    placed = (
        P("rhs", "wide"),
        P("rhs", "wide"),
        P("wide", None),
        P("wide", None),
        P("wide", None),
        P(),
        P(),
    )
    return jax.shard_map(
        on_device,
        mesh=mesh,
        in_specs=placed,
        out_specs=(P("rhs", "wide"), P("rhs", "wide")),
        check_vma=False,
    )
```
